256 devices in a mesh: tm: 32 (over x, y, core), group: 8 (over z).
Axes of the slice: x: 4, y: 4, z: 8, core: 2. Of those that a mesh axis runs over, the one named last changes fastest.
Arguments:
- frames: bfloat16 [8, 262144, 512], P('group', 'tm')
- pair_count: int32 [8], P('group'), may hold values from 131072 to 260096, as said below
Outputs:
- group_instant: float32 [8, 512, 512], P('group', 'tm')
- group_lagged: float32 [8, 512, 512], P('group', 'tm')
- pooled_instant: float32 [512, 512], P('tm')
- pooled_lagged: float32 [512, 512], P('tm')
The draws below stay inside these ranges and needn't reach their ends.
Inputs may be any that keep to these rules, and one draw needn't show every extreme that they name: `pair_count`: every session has between 131072 and 260096 pairs, and some session has exactly 260096.
All inputs are finite; a program needn't handle non-finite values.
Results may differ from the reference program's by a relative error of at most 0.0003.
Values may be sent and summed in bfloat16 or wider, within the bound.
No kernel may reach another device: no remote copies, remote signals or barrier semaphores. Data moves between devices by JAX's collectives and lax.ppermute only.
A program may use at most 64 MiB of HBM per device.

```python
import math
import jax
import jax.numpy as jnp
from jax import lax

F = 512
LAG = 2048
FRAMES_SEQ = 262144
GROUPS = 8


def draw_frames(key, part):
    modes = 64
    keys = jax.random.split(key, 5)
    freq = jnp.exp(jax.random.uniform(keys[0], (modes,), jnp.float32, math.log(2.0 * math.pi / (4.0 * LAG)), math.log(2.0 * math.pi / 16.0)))
    phase = jax.random.uniform(keys[1], (GROUPS, modes), jnp.float32, 0.0, 2.0 * math.pi)
    mixing = jax.random.normal(keys[2], (modes, F), jnp.float32) / math.sqrt(128.0)
    offset = 0.5 * jax.random.normal(keys[3], (GROUPS, F), jnp.float32)
    times = jnp.arange(FRAMES_SEQ, dtype=jnp.float32)
    envelope = 1.0 + 2.0 * times / FRAMES_SEQ

    def one_session(index):
        waves = jnp.sin(times[:, None] * freq[None] + phase[index][None])
        signal = jnp.dot(waves, mixing) * envelope[:, None]
        noise = jax.random.normal(jax.random.fold_in(keys[4], index), (FRAMES_SEQ, F), jnp.float32)
        return (signal + noise + offset[index][None]).astype(jnp.bfloat16)
    return lax.map(one_session, jnp.arange(GROUPS, dtype=jnp.int32))


def draw_pair_count(key, part):
    keys = jax.random.split(jax.random.fold_in(key, 17), 2)
    lowest = FRAMES_SEQ // 2
    highest = FRAMES_SEQ - LAG
    values = jax.random.randint(keys[0], (GROUPS,), lowest, highest + 1, jnp.int32)
    which = jax.random.randint(keys[1], (), 0, GROUPS, jnp.int32)
    return jnp.where(jnp.arange(GROUPS, dtype=jnp.int32) == which, highest, values).astype(jnp.int32)


def setup_inputs(seed: int = 0) -> dict:
    arg_keys = jax.random.split(jax.random.key(seed), 3)
    frames = draw_frames(jax.random.fold_in(arg_keys[2], 71), 0)
    pair_count = draw_pair_count(jax.random.fold_in(arg_keys[2], 71), 0)
    return dict(frames=frames, pair_count=pair_count)


def per_group(item):
    block, count = item
    span = FRAMES_SEQ - LAG
    wide = block[:span].astype(jnp.float32)
    later = block[LAG:].astype(jnp.float32)
    weight = (jnp.arange(span, dtype=jnp.int32) < count).astype(jnp.float32)[:, None]
    number = count.astype(jnp.float32)
    sum_x = jnp.sum(wide * weight, axis=0)
    sum_y = jnp.sum(later * weight, axis=0)
    cent_x = (wide - sum_x / number) * weight
    cent_y = (later - sum_y / number) * weight
    inst = jnp.dot(cent_x.T, cent_x, precision=lax.Precision.HIGHEST, preferred_element_type=jnp.float32)
    lagm = jnp.dot(cent_x.T, cent_y, precision=lax.Precision.HIGHEST, preferred_element_type=jnp.float32)
    return inst, lagm, sum_x, sum_y


def reference(frames, pair_count):
    inst, lagm, sum_x, sum_y = lax.map(per_group, (frames, pair_count))
    number = pair_count.astype(jnp.float32)
    group_instant = inst / number[:, None, None]
    group_lagged = lagm / number[:, None, None]
    total = jnp.sum(number)
    mean_x = sum_x / number[:, None]
    mean_y = sum_y / number[:, None]
    glob_x = jnp.sum(sum_x, axis=0) / total
    glob_y = jnp.sum(sum_y, axis=0) / total
    dev_x = mean_x - glob_x[None]
    dev_y = mean_y - glob_y[None]
    spread_i = jnp.einsum("g,gi,gj->ij", number, dev_x, dev_x, precision=lax.Precision.HIGHEST)
    spread_l = jnp.einsum("g,gi,gj->ij", number, dev_x, dev_y, precision=lax.Precision.HIGHEST)
    pooled_instant = (jnp.sum(inst, axis=0) + spread_i) / total
    pooled_lagged = (jnp.sum(lagm, axis=0) + spread_l) / total
    return group_instant, group_lagged, pooled_instant, pooled_lagged
```

```python
import functools

import jax
import jax.numpy as jnp
from jax import lax
from jax.experimental import pallas as pl
from jax.experimental.pallas import tpu as pltpu
from jax.sharding import PartitionSpec as P

LAG = 2048
BLK = 1024
LANES = 128
F32 = jnp.float32
CONTRACT = (((0,), (0,)), ((), ()))
VMEM_LIMIT = 48 * 1024 * 1024


def rows_below(limit, shape):
    return lax.broadcasted_iota(jnp.int32, shape, 0) < limit


def keep_below(block, limit):
    wide = jnp.where(rows_below(limit, block.shape), block.astype(F32), 0.0)
    return wide.astype(block.dtype)


def write_chunks(core, acc, tail, keep_ref, send_ref):
    chips, _, _ = keep_ref.shape
    width = acc.shape[1]
    share = acc.shape[0] // (2 * chips)
    for out, which in ((keep_ref, core), (send_ref, 1 - core)):
        for chip in range(chips):
            first = pl.multiple_of((2 * chip + which) * share, share)
            for col in range(width // LANES):
                out[chip, col * share : (col + 1) * share, :] = acc[
                    pl.ds(first, share), col * LANES : (col + 1) * LANES
                ]
            out[chip, share * (width // LANES) :, :] = tail


def tail_rows(sums, valid):
    width = sums.shape[1]
    parts = [sums[:, c * LANES : (c + 1) * LANES] for c in range(width // LANES)]
    count = jnp.full((8 - len(parts), LANES), valid, jnp.int32).astype(F32)
    return jnp.concatenate([*parts, count], axis=0)


def instant_kernel(
    place, x_hbm, keep_ref, send_ref, sum_y_ref, xs, acc, sum_x, sum_y, sems
):
    core, base, count = place[0], place[1], place[2]
    rows = xs.shape[0]
    blocks = rows // BLK

    def copy(b):
        part = pl.ds(b * BLK, BLK)
        return pltpu.make_async_copy(x_hbm.at[part], xs.at[part], sems.at[b])

    for b in range(blocks):
        copy(b).start()
    acc[...] = jnp.zeros_like(acc)
    sum_x[...] = jnp.zeros_like(sum_x)
    sum_y[...] = jnp.zeros_like(sum_y)

    def column_sum(wide):
        return jnp.sum(wide, axis=0, keepdims=True)

    for b in range(blocks):
        copy(b).wait()
        first = base + b * BLK
        full = first + BLK <= count

        @pl.when(full)
        def _():
            block = xs[b * BLK : (b + 1) * BLK, :]
            acc[...] += lax.dot_general(block, block, CONTRACT, preferred_element_type=F32)
            total = column_sum(block.astype(F32))
            sum_x[...] += total
            sum_y[...] += total * jnp.where(first >= LAG, 1.0, 0.0)

        @pl.when(jnp.logical_and(jnp.logical_not(full), first < count + LAG))
        def _():
            block = xs[b * BLK : (b + 1) * BLK, :]
            wide = block.astype(F32)
            held = jnp.where(rows_below(count - first, wide.shape), wide, 0.0)
            acc[...] += lax.dot_general(
                held.astype(block.dtype), block, CONTRACT, preferred_element_type=F32
            )
            later = jnp.where(rows_below(count + LAG - first, wide.shape), wide, 0.0)
            sum_x[...] += column_sum(held)
            sum_y[...] += column_sum(later) * jnp.where(first >= LAG, 1.0, 0.0)

    valid = jnp.clip(count - base, 0, rows)
    write_chunks(core, acc, tail_rows(sum_x[...], valid), keep_ref, send_ref)
    sum_y_ref[...] = jnp.broadcast_to(sum_y[...], sum_y_ref.shape)


def lagged_kernel(
    place, x_hbm, y_hbm, w_hbm, sum_y_ref, keep_ref, send_ref, xs, ys, ws, acc, sems
):
    core, base, count = place[0], place[1], place[2]
    rows = xs.shape[0]
    blocks = rows // BLK
    ahead = LAG // BLK

    def copy(b):
        part = pl.ds(b * BLK, BLK)
        return pltpu.make_async_copy(x_hbm.at[part], xs.at[part], sems.at[b])

    from_next = pltpu.make_async_copy(y_hbm, ys, sems.at[blocks])
    from_last = pltpu.make_async_copy(w_hbm, ws, sems.at[blocks + 1])
    for b in range(blocks):
        copy(b).start()
    from_next.start()
    from_last.start()
    acc[...] = jnp.zeros_like(acc)

    def add(first, early, late):
        full = first + BLK <= count

        @pl.when(full)
        def _():
            acc[...] += lax.dot_general(
                early[...], late[...], CONTRACT, preferred_element_type=F32
            )

        @pl.when(jnp.logical_and(jnp.logical_not(full), first < count))
        def _():
            acc[...] += lax.dot_general(
                keep_below(early[...], count - first),
                late[...],
                CONTRACT,
                preferred_element_type=F32,
            )

    def part(b):
        return xs.at[pl.ds(b * BLK, BLK)]

    for b in range(ahead):
        copy(b).wait()
    for b in range(blocks - ahead):
        copy(b + ahead).wait()
        add(base + b * BLK, part(b), part(b + ahead))
    from_next.wait()
    add(base + (blocks - ahead) * BLK, part(blocks - ahead), ys)
    from_last.wait()
    add(base - BLK, ws, part(1))
    valid = jnp.clip(count - base, 0, rows)
    write_chunks(core, acc, tail_rows(sum_y_ref[0:1, :], valid), keep_ref, send_ref)


def row_of(rows):
    return jnp.concatenate([rows[c : c + 1, :] for c in range(rows.shape[0])], axis=1)


def centered(total, mean_rows, mean_cols, number, share, out_ref):
    for col in range(out_ref.shape[1] // LANES):
        lanes = slice(col * LANES, (col + 1) * LANES)
        block = total[col * share : (col + 1) * share, :]
        out_ref[:, lanes] = block / number - mean_rows * mean_cols[:, lanes]


def finish(total_i, total_l, first_row, inst_ref, lag_ref):
    share, width = inst_ref.shape
    cols = width // LANES
    tail = share * cols
    number = total_i[tail + cols : tail + cols + 1, 0:1]
    mean_x = row_of(total_i[tail : tail + cols, :]) / number
    mean_y = row_of(total_l[tail : tail + cols, :]) / number
    row = lax.broadcasted_iota(jnp.int32, (share, width), 0)
    col = lax.broadcasted_iota(jnp.int32, (share, width), 1)
    own = jnp.where(col == row + first_row, jnp.broadcast_to(mean_x, (share, width)), 0.0)
    mean_rows = jnp.sum(own, axis=1, keepdims=True)
    centered(total_i, mean_rows, mean_x, number, share, inst_ref)
    centered(total_l, mean_rows, mean_y, number, share, lag_ref)


def session_kernel(place, parts_ref, inst_ref, lag_ref, total_ref):
    total = jnp.sum(parts_ref[...], axis=0)
    half = total.shape[0] // 2
    total_ref[...] = jnp.broadcast_to(total[None], total_ref.shape)
    finish(total[:half], total[half:], place[3], inst_ref, lag_ref)


def pooled_kernel(place, parts_ref, inst_ref, lag_ref):
    total = jnp.sum(parts_ref[...], axis=0)
    half = total.shape[0] // 2
    finish(total[:half], total[half:], place[3], inst_ref, lag_ref)


def on_device(frames, pair_count):
    local = frames[0]
    rows, width = local.shape
    blocks = rows // BLK
    parts = lax.axis_size("tm")
    sessions = lax.axis_size("group")
    chips = parts // 2
    share = width // parts
    chunk = share * (width // LANES) + 8
    me = lax.axis_index("tm")
    core = me % 2
    place = jnp.stack([core, me * rows, pair_count[0], me * share]).astype(jnp.int32)

    back = [(i, i - 1) for i in range(1, parts)]
    forth = [(i, i + 1) for i in range(parts - 1)]
    from_next = lax.ppermute(local[:BLK], "tm", back)
    from_last = lax.ppermute(local[rows - BLK :], "tm", forth)

    smem = pl.BlockSpec(memory_space=pltpu.SMEM)
    vmem = pl.BlockSpec(memory_space=pltpu.VMEM)
    hbm = pl.BlockSpec(memory_space=pl.ANY)
    half = jax.ShapeDtypeStruct((chips, chunk, LANES), F32)
    params = pltpu.CompilerParams(vmem_limit_bytes=VMEM_LIMIT)

    def cost(flops, moved):
        return pl.CostEstimate(flops=flops, bytes_accessed=moved, transcendentals=0)

    work = 2 * rows * width * width
    keep_i, send_i, sum_y = pl.pallas_call(
        instant_kernel,
        out_shape=(half, half, jax.ShapeDtypeStruct((8, width), F32)),
        in_specs=[smem, hbm],
        out_specs=(vmem, vmem, vmem),
        scratch_shapes=[
            pltpu.VMEM((rows, width), local.dtype),
            pltpu.VMEM((width, width), F32),
            pltpu.VMEM((1, width), F32),
            pltpu.VMEM((1, width), F32),
            pltpu.SemaphoreType.DMA((blocks,)),
        ],
        compiler_params=params,
        cost_estimate=cost(work, 10 << 20),
        name="instant",
    )(place, local)
    keep_l, send_l = pl.pallas_call(
        lagged_kernel,
        out_shape=(half, half),
        in_specs=[smem, hbm, hbm, hbm, vmem],
        out_specs=(vmem, vmem),
        scratch_shapes=[
            pltpu.VMEM((rows, width), local.dtype),
            pltpu.VMEM((BLK, width), local.dtype),
            pltpu.VMEM((BLK, width), local.dtype),
            pltpu.VMEM((width, width), F32),
            pltpu.SemaphoreType.DMA((blocks + 2,)),
        ],
        compiler_params=params,
        cost_estimate=cost(work, 12 << 20),
        name="lagged",
    )(place, local, from_next, from_last, sum_y)

    swap = [(i, i ^ 1) for i in range(parts)]
    both_i = keep_i + lax.ppermute(send_i, "tm", swap)
    both_l = keep_l + lax.ppermute(send_l, "tm", swap)
    both = jnp.concatenate([both_i, both_l], axis=1)
    same_core = [[2 * i + c for i in range(chips)] for c in range(2)]
    met = lax.all_to_all(both, "tm", 0, 0, axis_index_groups=same_core, tiled=True)

    out = jax.ShapeDtypeStruct((share, width), F32)
    group_instant, group_lagged, total = pl.pallas_call(
        session_kernel,
        out_shape=(out, out, jax.ShapeDtypeStruct((sessions, 2 * chunk, LANES), F32)),
        in_specs=[smem, vmem],
        out_specs=(vmem, vmem, vmem),
        compiler_params=params,
        name="session",
    )(place, met)
    all_total = lax.all_to_all(total, "group", 0, 0, tiled=True)
    pooled_instant, pooled_lagged = pl.pallas_call(
        pooled_kernel,
        out_shape=(out, out),
        in_specs=[smem, vmem],
        out_specs=(vmem, vmem),
        compiler_params=params,
        name="pooled",
    )(place, all_total)
    return (group_instant[None], group_lagged[None], pooled_instant, pooled_lagged)


def solution(mesh):
    in_specs = (P("group", "tm", None), P("group"))
    out_specs = (P("group", "tm", None), P("group", "tm", None), P("tm", None), P("tm", None))
    return jax.shard_map(
        on_device, mesh=mesh, in_specs=in_specs, out_specs=out_specs, check_vma=False
    )
```

```python
import math

import jax
import jax.numpy as jnp
from jax import lax
from jax.experimental import pallas as pl
from jax.experimental.pallas import tpu as pltpu
from jax.sharding import PartitionSpec as P

LAG = 2048
BLK = 1024
LANES = 128
F32 = jnp.float32
CONTRACT = (((0,), (0,)), ((), ()))
VMEM_LIMIT = 48 * 1024 * 1024


def rows_below(limit, shape):
    return lax.broadcasted_iota(jnp.int32, shape, 0) < limit


def keep_below(block, limit):
    wide = jnp.where(rows_below(limit, block.shape), block.astype(F32), 0.0)
    return wide.astype(block.dtype)


def write_chunks(place, acc, tail, keep_ref, send_ref, x_first):
    core, my_x, my_y = place[0], place[4], place[5]
    side = keep_ref.shape[0]
    width = acc.shape[1]
    share = acc.shape[0] // (2 * side * side)
    for out, which in ((keep_ref, core), (send_ref, 1 - core)):
        for i in range(side):
            for j in range(side):
                far_x, far_y = (i, j) if x_first else (j, i)
                chip = lax.rem(my_x + far_x, side) * side + lax.rem(my_y + far_y, side)
                first = pl.multiple_of((2 * chip + which) * share, share)
                for col in range(width // LANES):
                    out[i, j, col * share : (col + 1) * share, :] = acc[
                        pl.ds(first, share), col * LANES : (col + 1) * LANES
                    ]
                out[i, j, share * (width // LANES) :, :] = tail


def tail_rows(sums, valid):
    width = sums.shape[1]
    parts = [sums[:, c * LANES : (c + 1) * LANES] for c in range(width // LANES)]
    count = jnp.full((8 - len(parts), LANES), valid, jnp.int32).astype(F32)
    return jnp.concatenate([*parts, count], axis=0)


def moments_kernel(
    place, x_hbm, keep_ref, send_ref, lag, sum_y_ref, xs, acc, sum_x, sum_y, sems
):
    base, count = place[1], place[2]
    rows = xs.shape[0]
    blocks = rows // BLK
    ahead = LAG // BLK

    def copy(b):
        part = pl.ds(b * BLK, BLK)
        return pltpu.make_async_copy(x_hbm.at[part], xs.at[part], sems.at[b])

    for b in range(blocks):
        copy(b).start()
    acc[...] = jnp.zeros_like(acc)
    lag[...] = jnp.zeros_like(lag)
    sum_x[...] = jnp.zeros_like(sum_x)
    sum_y[...] = jnp.zeros_like(sum_y)

    def column_sum(wide):
        return jnp.sum(wide, axis=0, keepdims=True)

    def multiply(b, early):
        turned = early.T
        acc[...] += jnp.dot(turned, xs[b * BLK : (b + 1) * BLK, :], preferred_element_type=F32)
        if b + ahead < blocks:
            late = xs[(b + ahead) * BLK : (b + ahead + 1) * BLK, :]
            lag[...] += jnp.dot(turned, late, preferred_element_type=F32)

    for b in range(ahead):
        copy(b).wait()
    for b in range(blocks):
        if b + ahead < blocks:
            copy(b + ahead).wait()
        first = base + b * BLK
        full = first + BLK <= count

        @pl.when(full)
        def _():
            block = xs[b * BLK : (b + 1) * BLK, :]
            multiply(b, block)
            total = column_sum(block.astype(F32))
            sum_x[...] += total
            sum_y[...] += total * jnp.where(first >= LAG, 1.0, 0.0)

        @pl.when(jnp.logical_and(jnp.logical_not(full), first < count + LAG))
        def _():
            wide = xs[b * BLK : (b + 1) * BLK, :].astype(F32)
            held = jnp.where(rows_below(count - first, wide.shape), wide, 0.0)
            multiply(b, held.astype(xs.dtype))
            later = jnp.where(rows_below(count + LAG - first, wide.shape), wide, 0.0)
            sum_x[...] += column_sum(held)
            sum_y[...] += column_sum(later) * jnp.where(first >= LAG, 1.0, 0.0)

    valid = jnp.clip(count - base, 0, rows)
    write_chunks(place, acc, tail_rows(sum_x[...], valid), keep_ref, send_ref, False)
    sum_y_ref[...] = jnp.broadcast_to(sum_y[...], sum_y_ref.shape)


def border_kernel(
    place, x_hbm, y_ref, w_ref, part_ref, sum_y_ref, keep_ref, send_ref, xs, acc, sems
):
    base, count = place[1], place[2]
    rows = x_hbm.shape[0]
    last = rows - LAG

    def copy(k, first):
        return pltpu.make_async_copy(x_hbm.at[pl.ds(first, BLK)], xs.at[k], sems.at[k])

    copies = [copy(0, last), copy(1, BLK)]
    for each in copies:
        each.start()
    for each in copies:
        each.wait()
    full = base + last + BLK <= count

    @pl.when(full)
    def _():
        acc[...] = (
            part_ref[...]
            + lax.dot_general(xs[0], y_ref[...], CONTRACT, preferred_element_type=F32)
            + lax.dot_general(w_ref[...], xs[1], CONTRACT, preferred_element_type=F32)
        )

    @pl.when(jnp.logical_not(full))
    def _():
        early = keep_below(xs[0], count - base - last)
        before = keep_below(w_ref[...], count - base + BLK)
        acc[...] = (
            part_ref[...]
            + lax.dot_general(early, y_ref[...], CONTRACT, preferred_element_type=F32)
            + lax.dot_general(before, xs[1], CONTRACT, preferred_element_type=F32)
        )

    valid = jnp.clip(count - base, 0, rows)
    write_chunks(place, acc, tail_rows(sum_y_ref[0:1, :], valid), keep_ref, send_ref, True)


def edges_kernel(x_hbm, top_ref, end_ref, sems):
    rows, height = x_hbm.shape[0], top_ref.shape[0]
    top = pltpu.make_async_copy(x_hbm.at[pl.ds(0, height)], top_ref, sems.at[0])
    end = pltpu.make_async_copy(x_hbm.at[pl.ds(rows - height, height)], end_ref, sems.at[1])
    top.start()
    end.start()
    top.wait()
    end.wait()


def pair_kernel(keep_ref, met_ref, *outs):
    for d, out in enumerate(outs):
        out[...] = keep_ref[d] + met_ref[d]


def line_kernel(*refs):
    side = len(refs) // 2
    ins, outs = refs[:side], refs[side:]
    for d, out in enumerate(outs):
        out[...] = (ins[0][d] + ins[1][d]) + (ins[2][d] + ins[3][d])


def row_of(rows):
    return jnp.concatenate([rows[c : c + 1, :] for c in range(rows.shape[0])], axis=1)


def centered(total, mean_rows, mean_cols, number, share, out_ref):
    for col in range(out_ref.shape[1] // LANES):
        lanes = slice(col * LANES, (col + 1) * LANES)
        block = total[col * share : (col + 1) * share, :]
        out_ref[:, lanes] = block / number - mean_rows * mean_cols[:, lanes]


def finish(total_i, total_l, first_row, inst_ref, lag_ref):
    share, width = inst_ref.shape
    cols = width // LANES
    tail = share * cols
    number = total_i[tail + cols : tail + cols + 1, 0:1]
    mean_x = row_of(total_i[tail : tail + cols, :]) / number
    mean_y = row_of(total_l[tail : tail + cols, :]) / number
    row = lax.broadcasted_iota(jnp.int32, (share, width), 0)
    col = lax.broadcasted_iota(jnp.int32, (share, width), 1)
    own = jnp.where(col == row + first_row, jnp.broadcast_to(mean_x, (share, width)), 0.0)
    mean_rows = jnp.sum(own, axis=1, keepdims=True)
    centered(total_i, mean_rows, mean_x, number, share, inst_ref)
    centered(total_l, mean_rows, mean_y, number, share, lag_ref)


def session_kernel(place, *refs):
    inst_ref, lag_ref, total_ref = refs[-3:]
    parts = refs[:-3]
    half = total_ref.shape[0] // 2
    side = len(parts) // 2
    for k in range(2):
        a, b, c, d = parts[k * side : (k + 1) * side]
        total_ref[k * half : (k + 1) * half, :] = (a[...] + b[...]) + (c[...] + d[...])
    finish(total_ref[:half], total_ref[half:], place[3], inst_ref, lag_ref)


def duo_kernel(a_ref, b_ref, out_ref):
    out_ref[...] = a_ref[...] + b_ref[...]


def pooled_kernel(place, a_ref, b_ref, inst_ref, lag_ref):
    total = a_ref[...] + b_ref[...]
    half = total.shape[0] // 2
    finish(total[:half], total[half:], place[3], inst_ref, lag_ref)


def on_device(frames, pair_count):
    local = frames[0]
    rows, width = local.shape
    blocks = rows // BLK
    parts = lax.axis_size("tm")
    sessions = lax.axis_size("group")
    side = math.isqrt(parts // 2)
    share = width // parts
    chunk = share * (width // LANES) + 8
    me = lax.axis_index("tm")
    numbers = [me % 2, me * rows, pair_count[0], me * share, me // (2 * side), (me // 2) % side]
    place = jnp.stack(numbers).astype(jnp.int32)

    smem = pl.BlockSpec(memory_space=pltpu.SMEM)
    vmem = pl.BlockSpec(memory_space=pltpu.VMEM)
    hbm = pl.BlockSpec(memory_space=pl.ANY)
    params = pltpu.CompilerParams(vmem_limit_bytes=VMEM_LIMIT)

    def floats(*shape):
        return jax.ShapeDtypeStruct(shape, F32)

    def call(kernel, name, ins, out_shape, scratch=(), flops=0, moved=0):
        specs = jax.tree.map(lambda _: vmem, out_shape)
        return pl.pallas_call(
            kernel,
            out_shape=out_shape,
            in_specs=[spec for _, spec in ins],
            out_specs=specs,
            scratch_shapes=list(scratch),
            compiler_params=params,
            cost_estimate=pl.CostEstimate(flops=flops, bytes_accessed=moved, transcendentals=0),
            name=name,
        )(*[operand for operand, _ in ins])

    def dma(n):
        return pltpu.SemaphoreType.DMA((n,))

    where, frames_in = (place, smem), (local, hbm)
    edge = jax.ShapeDtypeStruct((BLK, width), local.dtype)
    top, end = pl.pallas_call(
        edges_kernel,
        out_shape=(edge, edge),
        in_specs=[hbm],
        out_specs=(vmem, vmem),
        scratch_shapes=[dma(2)],
        compiler_params=params,
        name="edges",
    )(local)
    back = [(i, i - 1) for i in range(1, parts)]
    forth = [(i, i + 1) for i in range(parts - 1)]
    from_next = lax.ppermute(top, "tm", back)
    from_last = lax.ppermute(end, "tm", forth)

    swap = [(i, i ^ 1) for i in range(parts)]

    def at(x, y, c):
        return ((x % side) * side + y % side) * 2 + c

    def along(block, far_x, far_y):
        grid = [(x, y, c) for x in range(side) for y in range(side) for c in range(2)]
        route = [(at(x, y, c), at(x + far_x, y + far_y, c)) for x, y, c in grid]
        return lax.ppermute(block, "tm", route)

    def gather(blocks, on_x):
        moved = [along(blocks[d], d * on_x, d * (1 - on_x)) for d in range(1, side)]
        return [blocks[0], *moved]

    def over_plane(keep, send, x_first, name):
        met = lax.ppermute(send, "tm", swap)
        lines = call(pair_kernel, "pair_" + name, [(keep, vmem), (met, vmem)], [floats(side, chunk, LANES)] * side)
        came = gather(lines, x_first)
        cells = call(line_kernel, "line_" + name, [(v, vmem) for v in came], [floats(chunk, LANES)] * side)
        return gather(cells, 1 - x_first)

    half = floats(side, side, chunk, LANES)
    square = pltpu.VMEM((width, width), F32)
    held = pltpu.VMEM((rows, width), local.dtype)
    line = pltpu.VMEM((1, width), F32)
    work = 2 * rows * width * width
    keep_i, send_i, partial, sum_y = call(
        moments_kernel,
        "moments",
        [where, frames_in],
        (half, half, floats(width, width), floats(8, width)),
        [held, square, line, line, dma(blocks)],
        work * 7 // 4,
        rows * width * 2,
    )
    keep_l, send_l = call(
        border_kernel,
        "border",
        [where, frames_in, (from_next, vmem), (from_last, vmem), (partial, vmem), (sum_y, vmem)],
        (half, half),
        [pltpu.VMEM((2, BLK, width), local.dtype), square, dma(2)],
        work // 4,
        rows * width,
    )
    cells_i = over_plane(keep_i, send_i, 0, "instant")
    cells_l = over_plane(keep_l, send_l, 1, "lagged")
    out = floats(share, width)
    group_instant, group_lagged, total = call(
        session_kernel,
        "session",
        [where, *[(v, vmem) for v in (*cells_i, *cells_l)]],
        (out, out, floats(2 * chunk, LANES)),
    )
    for route in (lambda i: i ^ 1, lambda i: i ^ 2, lambda i: (sessions - 2 - (i & -2)) | (i & 1)):
        other = lax.ppermute(total, "group", [(i, route(i)) for i in range(sessions)])
        last = (total, other)
        total = call(duo_kernel, "duo", [(v, vmem) for v in last], floats(2 * chunk, LANES))
    pooled_instant, pooled_lagged = call(
        pooled_kernel, "pooled", [where, *[(v, vmem) for v in last]], (out, out)
    )
    return (group_instant[None], group_lagged[None], pooled_instant, pooled_lagged)


def solution(mesh):
    in_specs = (P("group", "tm", None), P("group"))
    out_specs = (P("group", "tm", None), P("group", "tm", None), P("tm", None), P("tm", None))
    return jax.shard_map(
        on_device, mesh=mesh, in_specs=in_specs, out_specs=out_specs, check_vma=False
    )
```

```python
import functools
import math

import jax
import jax.numpy as jnp
from jax import lax
from jax.experimental import pallas as pl
from jax.experimental.pallas import tpu as pltpu
from jax.sharding import PartitionSpec as P

LAG = 2048
BLK = 1024
LANES = 128
F32 = jnp.float32
CONTRACT = (((0,), (0,)), ((), ()))
VMEM_LIMIT = 47 * 1024 * 1024


def rows_below(limit, shape):
    return lax.broadcasted_iota(jnp.int32, shape, 0) < limit


def keep_below(block, limit):
    wide = jnp.where(rows_below(limit, block.shape), block.astype(F32), 0.0)
    return wide.astype(block.dtype)


def write_chunks(place, acc, tail, keep_ref, send_ref, x_first):
    core, my_x, my_y = place[0], place[4], place[5]
    side = keep_ref.shape[0]
    width = acc.shape[1]
    share = acc.shape[0] // (2 * side * side)
    for out, which in ((keep_ref, core), (send_ref, 1 - core)):
        for i in range(side):
            for j in range(side):
                far_x, far_y = (i, j) if x_first else (j, i)
                chip = lax.rem(my_x + far_x, side) * side + lax.rem(my_y + far_y, side)
                first = pl.multiple_of((2 * chip + which) * share, share)
                for col in range(width // LANES):
                    out[i, j, col * share : (col + 1) * share, :] = acc[
                        pl.ds(first, share), col * LANES : (col + 1) * LANES
                    ]
                out[i, j, share * (width // LANES) :, :] = tail


def tail_rows(sums, valid):
    width = sums.shape[1]
    parts = [sums[:, c * LANES : (c + 1) * LANES] for c in range(width // LANES)]
    count = jnp.full((8 - len(parts), LANES), valid, jnp.int32).astype(F32)
    return jnp.concatenate([*parts, count], axis=0)


def fold(wide):
    return jnp.sum(wide.reshape(-1, 8, wide.shape[1]), axis=0)


def dot(early, late):
    return lax.dot_general(early, late, CONTRACT, preferred_element_type=F32)


def add_whole(block_ref, first, acc, sums, pair):
    block = block_ref[...]
    acc[...] += dot(block, block)
    if pair is not None:
        pair[0][...] += dot(pair[1][...], block)
    total = fold(block.astype(F32))
    sums[0:8, :] += total
    sums[8:16, :] += total * jnp.where(first >= LAG, 1.0, 0.0)


def add_block(block_ref, first, count, acc, sums, pair):
    full = first + BLK <= count

    @pl.when(full)
    def _():
        add_whole(block_ref, first, acc, sums, pair)

    @pl.when(jnp.logical_and(jnp.logical_not(full), first < count + LAG))
    def _():
        block = block_ref[...]
        wide = block.astype(F32)
        held = jnp.where(rows_below(count - first, wide.shape), wide, 0.0)
        acc[...] += dot(held.astype(block.dtype), block)
        if pair is not None:
            pair[0][...] += dot(keep_below(pair[1][...], count - first + LAG), block)
        later = jnp.where(rows_below(count + LAG - first, wide.shape), wide, 0.0)
        sums[0:8, :] += fold(held)
        sums[8:16, :] += fold(later) * jnp.where(first >= LAG, 1.0, 0.0)


def edge_kernel(which, place, x_hbm, out_ref, sems):
    rows, height = x_hbm.shape[0], out_ref.shape[0]
    parts = sems.shape[0]
    step = height // parts
    start = jnp.where(place[0] == which, rows - height, 0)
    copies = []
    for k in range(parts):
        first = pl.multiple_of(start + k * step, step)
        source = x_hbm.at[pl.ds(first, step)]
        copies.append(pltpu.make_async_copy(source, out_ref.at[pl.ds(k * step, step)], sems.at[k]))
    for copy in copies:
        copy.start()
    for copy in copies:
        copy.wait()


def moments_kernel(
    place, x_hbm, keep_ref, send_ref, lag, sum_y_ref, second_ref, late_ref, xs, acc, sums, sems
):
    base, count = place[1], place[2]
    rows = x_hbm.shape[0]
    blocks = rows // BLK
    ahead = LAG // BLK

    def copy(b):
        return pltpu.make_async_copy(x_hbm.at[pl.ds(b * BLK, BLK)], xs.at[b], sems.at[b])

    def again(k, b, out):
        return pltpu.make_async_copy(x_hbm.at[pl.ds(b * BLK, BLK)], out, sems.at[blocks + k])

    kept = [again(0, 1, second_ref), again(1, blocks - ahead, late_ref)]
    for b in range(blocks):
        copy(b).start()
    for each in kept:
        each.start()
    acc[...] = jnp.zeros_like(acc)
    sums[...] = jnp.zeros_like(sums)
    lag[...] = jnp.zeros_like(lag)

    def step(b, with_pair):
        copy(b).wait()
        pair = (lag, xs.at[b - ahead]) if with_pair else None
        add_block(xs.at[b], base + b * BLK, count, acc, sums, pair)

    pl.loop(0, ahead)(lambda b: step(b, False))
    pl.loop(ahead, blocks)(lambda b: step(b, True))
    for each in kept:
        each.wait()
    valid = jnp.clip(count - base, 0, rows)
    sum_x = jnp.sum(sums[0:8, :], axis=0, keepdims=True)
    sum_y = jnp.sum(sums[8:16, :], axis=0, keepdims=True)
    write_chunks(place, acc, tail_rows(sum_x, valid), keep_ref, send_ref, True)
    sum_y_ref[...] = jnp.broadcast_to(sum_y, sum_y_ref.shape)


def border_kernel(
    place, far_ref, near_ref, second_ref, late_ref, part_ref, sum_y_ref, keep_ref, send_ref, acc
):
    core, base, count = place[0], place[1], place[2]
    rows = place[6]
    first = base + rows - LAG

    def add(next_ref, last_ref):
        full = first + BLK <= count

        @pl.when(full)
        def _():
            acc[...] = (
                part_ref[...] + dot(late_ref[...], next_ref[...]) + dot(last_ref[...], second_ref[...])
            )

        @pl.when(jnp.logical_not(full))
        def _():
            early = keep_below(late_ref[...], count - first)
            before = keep_below(last_ref[...], count - base + BLK)
            acc[...] = part_ref[...] + dot(early, next_ref[...]) + dot(before, second_ref[...])

    @pl.when(core == 1)
    def _():
        add(far_ref, near_ref)

    @pl.when(core == 0)
    def _():
        add(near_ref, far_ref)

    valid = jnp.clip(count - base, 0, rows)
    write_chunks(place, acc, tail_rows(sum_y_ref[0:1, :], valid), keep_ref, send_ref, False)


def pair_kernel(keep_ref, met_ref, *outs):
    for d, out in enumerate(outs):
        out[...] = keep_ref[d] + met_ref[d]


def line_kernel(*refs):
    side = len(refs) // 2
    ins, outs = refs[:side], refs[side:]
    for d, out in enumerate(outs):
        out[...] = (ins[0][d] + ins[1][d]) + (ins[2][d] + ins[3][d])


def row_of(rows):
    return jnp.concatenate([rows[c : c + 1, :] for c in range(rows.shape[0])], axis=1)


def centered(total, mean_rows, mean_cols, number, share, out_ref):
    for col in range(out_ref.shape[1] // LANES):
        lanes = slice(col * LANES, (col + 1) * LANES)
        block = total[col * share : (col + 1) * share, :]
        out_ref[:, lanes] = block / number - mean_rows * mean_cols[:, lanes]


def finish(total_i, total_l, first_row, inst_ref, lag_ref):
    share, width = inst_ref.shape
    cols = width // LANES
    tail = share * cols
    number = total_i[tail + cols : tail + cols + 1, 0:1]
    mean_x = row_of(total_i[tail : tail + cols, :]) / number
    mean_y = row_of(total_l[tail : tail + cols, :]) / number
    row = lax.broadcasted_iota(jnp.int32, (share, width), 0)
    col = lax.broadcasted_iota(jnp.int32, (share, width), 1)
    own = jnp.where(col == row + first_row, jnp.broadcast_to(mean_x, (share, width)), 0.0)
    mean_rows = jnp.sum(own, axis=1, keepdims=True)
    centered(total_i, mean_rows, mean_x, number, share, inst_ref)
    centered(total_l, mean_rows, mean_y, number, share, lag_ref)


def plane_kernel(*refs):
    *parts, total_ref = refs
    half = total_ref.shape[0] // 2
    side = len(parts) // 2
    for k in range(2):
        a, b, c, d = parts[k * side : (k + 1) * side]
        total_ref[k * half : (k + 1) * half, :] = (a[...] + b[...]) + (c[...] + d[...])


def session_kernel(place, total_ref, inst_ref, lag_ref):
    half = total_ref.shape[0] // 2
    finish(total_ref[:half], total_ref[half:], place[3], inst_ref, lag_ref)


def duo_kernel(a_ref, b_ref, out_ref):
    out_ref[...] = a_ref[...] + b_ref[...]


def pooled_kernel(place, a_ref, b_ref, inst_ref, lag_ref):
    total = a_ref[...] + b_ref[...]
    half = total.shape[0] // 2
    finish(total[:half], total[half:], place[3], inst_ref, lag_ref)


def on_device(frames, pair_count):
    local = frames[0]
    rows, width = local.shape
    blocks = rows // BLK
    parts = lax.axis_size("tm")
    sessions = lax.axis_size("group")
    side = math.isqrt(parts // 2)
    share = width // parts
    chunk = share * (width // LANES) + 8
    me = lax.axis_index("tm")
    numbers = [me % 2, me * rows, pair_count[0], me * share, me // (2 * side), (me // 2) % side, rows]
    place = jnp.stack(numbers).astype(jnp.int32)

    smem = pl.BlockSpec(memory_space=pltpu.SMEM)
    vmem = pl.BlockSpec(memory_space=pltpu.VMEM)
    hbm = pl.BlockSpec(memory_space=pl.ANY)
    params = pltpu.CompilerParams(vmem_limit_bytes=VMEM_LIMIT)

    def floats(*shape):
        return jax.ShapeDtypeStruct(shape, F32)

    def call(kernel, name, ins, out_shape, scratch=(), flops=0, moved=0):
        specs = jax.tree.map(lambda _: vmem, out_shape)
        return pl.pallas_call(
            kernel,
            out_shape=out_shape,
            in_specs=[spec for _, spec in ins],
            out_specs=specs,
            scratch_shapes=list(scratch),
            compiler_params=params,
            cost_estimate=pl.CostEstimate(flops=flops, bytes_accessed=moved, transcendentals=0),
            name=name,
        )(*[operand for operand, _ in ins])

    def dma(n):
        return pltpu.SemaphoreType.DMA((n,))

    where, frames_in = (place, smem), (local, hbm)
    edge = jax.ShapeDtypeStruct((BLK, width), local.dtype)
    swap = [(i, i ^ 1) for i in range(parts)]
    cross = [(i, i + 1 if i % 2 else i - 1) for i in range(1, parts - 1)]

    def neighbours(which, route, name):
        kernel = functools.partial(edge_kernel, which)
        block = call(kernel, name, [where, frames_in], edge, [dma(4)], 0, 2 * BLK * width)
        return lax.ppermute(block, "tm", route)

    far = neighbours(1, cross, "edge_far")
    near = neighbours(0, swap, "edge_near")

    def at(x, y, c):
        return ((x % side) * side + y % side) * 2 + c

    def along(block, far_x, far_y):
        grid = [(x, y, c) for x in range(side) for y in range(side) for c in range(2)]
        route = [(at(x, y, c), at(x + far_x, y + far_y, c)) for x, y, c in grid]
        return lax.ppermute(block, "tm", route)

    def gather(blocks, on_x):
        moved = [along(blocks[d], d * on_x, d * (1 - on_x)) for d in range(1, side)]
        return [blocks[0], *moved]

    def over_pair(keep, send, name):
        met = lax.ppermute(send, "tm", swap)
        return call(pair_kernel, "pair_" + name, [(keep, vmem), (met, vmem)], [floats(side, chunk, LANES)] * side)

    def over_plane(lines, x_first, name):
        came = gather(lines, x_first)
        cells = call(line_kernel, "line_" + name, [(v, vmem) for v in came], [floats(chunk, LANES)] * side)
        return gather(cells, 1 - x_first)

    half = floats(side, side, chunk, LANES)
    square = pltpu.VMEM((width, width), F32)
    held = pltpu.VMEM((blocks, BLK, width), local.dtype)
    work = 2 * rows * width * width
    keep_i, send_i, partial, sum_y, second, late = call(
        moments_kernel,
        "moments",
        [where, frames_in],
        (half, half, floats(width, width), floats(8, width), edge, edge),
        [held, square, pltpu.VMEM((16, width), F32), dma(blocks + 2)],
        work * 7 // 4,
        rows * width * 2,
    )
    keep_l, send_l = call(
        border_kernel,
        "border",
        [where, *[(v, vmem) for v in (far, near, second, late, partial, sum_y)]],
        (half, half),
        [square],
        work // 4,
        rows * width,
    )
    lines_i = over_pair(keep_i, send_i, "instant")
    cells_i = over_plane(lines_i, 1, "instant")
    cells_l = over_plane(over_pair(keep_l, send_l, "lagged"), 0, "lagged")
    out = floats(share, width)
    total = call(plane_kernel, "plane", [(v, vmem) for v in (*cells_i, *cells_l)], floats(2 * chunk, LANES))
    group_instant, group_lagged = call(session_kernel, "session", [where, (total, vmem)], (out, out))
    for route in (lambda i: i ^ 1, lambda i: i ^ 2, lambda i: (sessions - 2 - (i & -2)) | (i & 1)):
        other = lax.ppermute(total, "group", [(i, route(i)) for i in range(sessions)])
        last = (total, other)
        total = call(duo_kernel, "duo", [(v, vmem) for v in last], floats(2 * chunk, LANES))
    pooled_instant, pooled_lagged = call(
        pooled_kernel, "pooled", [where, *[(v, vmem) for v in last]], (out, out)
    )
    return (group_instant[None], group_lagged[None], pooled_instant, pooled_lagged)


def solution(mesh):
    in_specs = (P("group", "tm", None), P("group"))
    out_specs = (P("group", "tm", None), P("group", "tm", None), P("tm", None), P("tm", None))
    return jax.shard_map(
        on_device, mesh=mesh, in_specs=in_specs, out_specs=out_specs, check_vma=False
    )
```

```python
import math

import jax
import jax.numpy as jnp
from jax import lax
from jax.experimental import pallas as pl
from jax.experimental.pallas import tpu as pltpu
from jax.sharding import PartitionSpec as P

LAG = 2048
BLK = 1024
LANES = 128
F32 = jnp.float32
CONTRACT = (((0,), (0,)), ((), ()))
VMEM_LIMIT = 47 * 1024 * 1024


def rows_below(limit, shape):
    return lax.broadcasted_iota(jnp.int32, shape, 0) < limit


def keep_below(block, limit):
    wide = jnp.where(rows_below(limit, block.shape), block.astype(F32), 0.0)
    return wide.astype(block.dtype)


def write_chunks(place, acc, tail, keep_ref, send_ref):
    core, my_x, my_y = place[0], place[4], place[5]
    side = keep_ref.shape[0]
    width = acc.shape[1]
    share = acc.shape[0] // (2 * side * side)
    for out, which in ((keep_ref, core), (send_ref, 1 - core)):
        for i in range(side):
            for j in range(side):
                far_x = jnp.where(which == 1, i, j)
                far_y = jnp.where(which == 1, j, i)
                chip = lax.rem(my_x + far_x, side) * side + lax.rem(my_y + far_y, side)
                first = pl.multiple_of((2 * chip + which) * share, share)
                for col in range(width // LANES):
                    out[i, j, col * share : (col + 1) * share, :] = acc[
                        pl.ds(first, share), col * LANES : (col + 1) * LANES
                    ]
                if tail is not None:
                    out[i, j, share * (width // LANES) :, :] = tail


def tail_rows(*sums):
    return jnp.concatenate(
        [each[:, c * LANES : (c + 1) * LANES] for each in sums for c in range(each.shape[1] // LANES)], axis=0
    )


def fold(wide):
    return jnp.sum(wide.reshape(-1, 8, wide.shape[1]), axis=0)


def dot(early, late):
    return lax.dot_general(early, late, CONTRACT, preferred_element_type=F32)


def add_whole(block_ref, first, acc, sums, pair):
    block = block_ref[...]
    acc[...] += dot(block, block)
    if pair is not None:
        pair[0][...] += dot(pair[1][...], block)
    total = fold(block.astype(F32))
    sums[0:8, :] += total
    sums[8:16, :] += total * jnp.where(first >= LAG, 1.0, 0.0)


def add_block(block_ref, first, count, acc, sums, pair):
    full = first + BLK <= count

    @pl.when(full)
    def _():
        add_whole(block_ref, first, acc, sums, pair)

    @pl.when(jnp.logical_and(jnp.logical_not(full), first < count + LAG))
    def _():
        block = block_ref[...]
        wide = block.astype(F32)
        held = jnp.where(rows_below(count - first, wide.shape), wide, 0.0)
        acc[...] += dot(held.astype(block.dtype), block)
        if pair is not None:
            pair[0][...] += dot(keep_below(pair[1][...], count - first + LAG), block)
        later = jnp.where(rows_below(count + LAG - first, wide.shape), wide, 0.0)
        sums[0:8, :] += fold(held)
        sums[8:16, :] += fold(later) * jnp.where(first >= LAG, 1.0, 0.0)


def edges_kernel(place, x_hbm, far_ref, near_ref, sems):
    rows, height = x_hbm.shape[0], far_ref.shape[0]
    parts = sems.shape[0] // 2
    step = height // parts
    copies = []
    for which, out in ((1, far_ref), (0, near_ref)):
        start = jnp.where(place[0] == which, rows - height, 0)
        for k in range(parts):
            source = x_hbm.at[pl.ds(pl.multiple_of(start + k * step, step), step)]
            sem = sems.at[which * parts + k]
            copies.append(pltpu.make_async_copy(source, out.at[pl.ds(k * step, step)], sem))
    for copy in copies:
        copy.start()
    for copy in copies:
        copy.wait()


def moments_kernel(
    place, x_hbm, keep_ref, send_ref, lag, second_ref, late_ref, facts_ref, xs, acc, sums, sems
):
    base, count = place[1], place[2]
    rows = x_hbm.shape[0]
    blocks = rows // BLK
    ahead = LAG // BLK

    def copy(b):
        return pltpu.make_async_copy(x_hbm.at[pl.ds(b * BLK, BLK)], xs.at[b], sems.at[b])

    def again(k, b, out):
        return pltpu.make_async_copy(x_hbm.at[pl.ds(b * BLK, BLK)], out, sems.at[blocks + k])

    kept = [again(0, 1, second_ref), again(1, blocks - ahead, late_ref)]
    for b in range(blocks):
        copy(b).start()
    for each in kept:
        each.start()
    acc[...] = jnp.zeros_like(acc)
    sums[...] = jnp.zeros_like(sums)
    lag[...] = jnp.zeros_like(lag)

    def step(b, with_pair):
        copy(b).wait()
        pair = (lag, xs.at[b - ahead]) if with_pair else None
        add_block(xs.at[b], base + b * BLK, count, acc, sums, pair)

    pl.loop(0, ahead)(lambda b: step(b, False))
    pl.loop(ahead, blocks)(lambda b: step(b, True))
    for each in kept:
        each.wait()
    sum_x = jnp.sum(sums[0:8, :], axis=0, keepdims=True)
    sum_y = jnp.sum(sums[8:16, :], axis=0, keepdims=True)
    write_chunks(place, acc, tail_rows(sum_x, sum_y), keep_ref, send_ref)
    facts_ref[0:8, :] = jnp.full((8, LANES), count, jnp.int32).astype(F32)
    facts_ref[8:16, :] = jnp.full((8, LANES), place[3], jnp.int32).astype(F32)


def border_kernel(
    place, far_ref, near_ref, second_ref, late_ref, part_ref, keep_ref, send_ref, acc
):
    core, base, count = place[0], place[1], place[2]
    rows = place[6]
    first = base + rows - LAG

    def add(next_ref, last_ref):
        full = first + BLK <= count

        @pl.when(full)
        def _():
            acc[...] = (
                part_ref[...] + dot(late_ref[...], next_ref[...]) + dot(last_ref[...], second_ref[...])
            )

        @pl.when(jnp.logical_not(full))
        def _():
            early = keep_below(late_ref[...], count - first)
            before = keep_below(last_ref[...], count - base + BLK)
            acc[...] = part_ref[...] + dot(early, next_ref[...]) + dot(before, second_ref[...])

    @pl.when(core == 1)
    def _():
        add(far_ref, near_ref)

    @pl.when(core == 0)
    def _():
        add(near_ref, far_ref)

    write_chunks(place, acc, None, keep_ref, send_ref)


def pair_kernel(keep_i, met_i, keep_l, met_l, *outs):
    half = keep_i.shape[2]
    for d, out in enumerate(outs):
        out[:, :half, :] = keep_i[d] + met_i[d]
        out[:, half:, :] = keep_l[d] + met_l[d]


def line_kernel(a_ref, b_ref, c_ref, d_ref, *outs):
    for d, out in enumerate(outs):
        out[...] = (a_ref[d] + b_ref[d]) + (c_ref[d] + d_ref[d])


def plane_kernel(facts_ref, a_ref, b_ref, c_ref, d_ref, total_ref):
    height = a_ref.shape[0]
    total_ref[:height, :] = (a_ref[...] + b_ref[...]) + (c_ref[...] + d_ref[...])
    total_ref[height:, :] = facts_ref[0:8, :]


def row_of(rows):
    return jnp.concatenate([rows[c : c + 1, :] for c in range(rows.shape[0])], axis=1)


def centered(total, mean_rows, mean_cols, number, share, out_ref):
    for col in range(out_ref.shape[1] // LANES):
        lanes = slice(col * LANES, (col + 1) * LANES)
        block = total[col * share : (col + 1) * share, :]
        out_ref[:, lanes] = block / number - mean_rows * mean_cols[:, lanes]


def finish(total, facts_ref, inst_ref, lag_ref):
    share, width = inst_ref.shape
    cols = width // LANES
    flat = share * cols
    after = flat + 2 * cols
    number = total[flat + after : flat + after + 1, 0:1]
    mean_x = row_of(total[flat : flat + cols, :]) / number
    mean_y = row_of(total[flat + cols : after, :]) / number
    row = lax.broadcasted_iota(jnp.int32, (share, width), 0)
    col = lax.broadcasted_iota(jnp.int32, (share, width), 1)
    first_row = facts_ref[8:9, 0:1].astype(jnp.int32)
    own = jnp.where(col - row == jnp.broadcast_to(first_row, row.shape), jnp.broadcast_to(mean_x, (share, width)), 0.0)
    mean_rows = jnp.sum(own, axis=1, keepdims=True)
    centered(total[:flat, :], mean_rows, mean_x, number, share, inst_ref)
    centered(total[after : after + flat, :], mean_rows, mean_y, number, share, lag_ref)


def session_kernel(facts_ref, total_ref, inst_ref, lag_ref):
    finish(total_ref[...], facts_ref, inst_ref, lag_ref)


def duo_kernel(a_ref, b_ref, out_ref):
    out_ref[...] = a_ref[...] + b_ref[...]


def pooled_kernel(facts_ref, a_ref, b_ref, inst_ref, lag_ref):
    finish(a_ref[...] + b_ref[...], facts_ref, inst_ref, lag_ref)


def on_device(frames, pair_count):
    local = frames[0]
    rows, width = local.shape
    blocks = rows // BLK
    parts = lax.axis_size("tm")
    sessions = lax.axis_size("group")
    side = math.isqrt(parts // 2)
    share = width // parts
    flat = share * (width // LANES)
    tail = 2 * (width // LANES)
    chunk = 2 * flat + tail
    me = lax.axis_index("tm")
    numbers = [me % 2, me * rows, pair_count[0], me * share, me // (2 * side), (me // 2) % side, rows]
    place = jnp.stack(numbers).astype(jnp.int32)

    smem = pl.BlockSpec(memory_space=pltpu.SMEM)
    vmem = pl.BlockSpec(memory_space=pltpu.VMEM)
    hbm = pl.BlockSpec(memory_space=pl.ANY)
    params = pltpu.CompilerParams(vmem_limit_bytes=VMEM_LIMIT)

    def floats(*shape):
        return jax.ShapeDtypeStruct(shape, F32)

    def call(kernel, name, ins, out_shape, scratch=(), flops=0, moved=0):
        specs = jax.tree.map(lambda _: vmem, out_shape)
        return pl.pallas_call(
            kernel,
            out_shape=out_shape,
            in_specs=[spec for _, spec in ins],
            out_specs=specs,
            scratch_shapes=list(scratch),
            compiler_params=params,
            cost_estimate=pl.CostEstimate(flops=flops, bytes_accessed=moved, transcendentals=0),
            name=name,
        )(*[operand for operand, _ in ins])

    def dma(n):
        return pltpu.SemaphoreType.DMA((n,))

    where, frames_in = (place, smem), (local, hbm)
    edge = jax.ShapeDtypeStruct((BLK, width), local.dtype)
    swap = [(i, i ^ 1) for i in range(parts)]
    cross = [(i, i + 1 if i % 2 else i - 1) for i in range(1, parts - 1)]

    far, near = call(edges_kernel, "edges", [where, frames_in], (edge, edge), [dma(8)], 0, 4 * BLK * width)
    far = lax.ppermute(far, "tm", cross)
    near = lax.ppermute(near, "tm", swap)

    def at(x, y, c):
        return ((x % side) * side + y % side) * 2 + c

    def gather(blocks, stage):
        came = [blocks[0]]
        for d in range(1, side):
            route = []
            for x in range(side):
                for y in range(side):
                    for c in range(2):
                        on_x = c != stage
                        route.append((at(x, y, c), at(x + d * on_x, y + d * (not on_x), c)))
            came.append(lax.ppermute(blocks[d], "tm", route))
        return came

    square = pltpu.VMEM((width, width), F32)
    held = pltpu.VMEM((blocks, BLK, width), local.dtype)
    work = 2 * rows * width * width
    keep_i, send_i, partial, second, late, facts = call(
        moments_kernel,
        "moments",
        [where, frames_in],
        (*[floats(side, side, flat + tail, LANES)] * 2, floats(width, width), edge, edge, floats(16, LANES)),
        [held, square, pltpu.VMEM((16, width), F32), dma(blocks + 2)],
        work * 7 // 4,
        rows * width * 2,
    )
    keep_l, send_l = call(
        border_kernel,
        "border",
        [where, *[(v, vmem) for v in (far, near, second, late, partial)]],
        [floats(side, side, flat, LANES)] * 2,
        [square],
        work // 4,
        rows * width,
    )
    met_i = lax.ppermute(send_i, "tm", swap)
    met_l = lax.ppermute(send_l, "tm", swap)

    def all_vmem(values):
        return [(v, vmem) for v in values]

    both = floats(side, chunk, LANES)
    lines = call(pair_kernel, "pair", all_vmem((keep_i, met_i, keep_l, met_l)), [both] * side)
    cells = call(line_kernel, "line", all_vmem(gather(lines, 0)), [floats(chunk, LANES)] * side)
    whole = floats(chunk + 8, LANES)
    total = call(plane_kernel, "plane", all_vmem((facts, *gather(cells, 1))), whole)
    out = floats(share, width)
    group_instant, group_lagged = call(session_kernel, "session", all_vmem((facts, total)), (out, out))
    for route in (lambda i: i ^ 1, lambda i: i ^ 2, lambda i: (sessions - 2 - (i & -2)) | (i & 1)):
        other = lax.ppermute(total, "group", [(i, route(i)) for i in range(sessions)])
        last = (total, other)
        total = call(duo_kernel, "duo", all_vmem(last), whole)
    pooled_instant, pooled_lagged = call(
        pooled_kernel, "pooled", all_vmem((facts, *last)), (out, out)
    )
    return (group_instant[None], group_lagged[None], pooled_instant, pooled_lagged)


def solution(mesh):
    in_specs = (P("group", "tm", None), P("group"))
    out_specs = (P("group", "tm", None), P("group", "tm", None), P("tm", None), P("tm", None))
    return jax.shard_map(
        on_device, mesh=mesh, in_specs=in_specs, out_specs=out_specs, check_vma=False
    )
```

```python
import functools
import math

import jax
import jax.numpy as jnp
from jax import lax
from jax.experimental import pallas as pl
from jax.experimental.pallas import tpu as pltpu
from jax.sharding import PartitionSpec as P

LAG = 2048
BLK = 1024
LANES = 128
F32 = jnp.float32
CONTRACT = (((0,), (0,)), ((), ()))
VMEM_LIMIT = 47 * 1024 * 1024


def rows_below(limit, shape):
    return lax.broadcasted_iota(jnp.int32, shape, 0) < limit


def keep_below(block, limit):
    wide = jnp.where(rows_below(limit, block.shape), block.astype(F32), 0.0)
    return wide.astype(block.dtype)


def write_chunks(place, acc, tail, keep_ref, send_ref):
    core, my_x, my_y = place[0], place[4], place[5]
    side = keep_ref.shape[0]
    width = acc.shape[1]
    share = acc.shape[0] // (2 * side * side)
    for out, which in ((keep_ref, core), (send_ref, 1 - core)):
        for i in range(side):
            for j in range(side):
                far_x = jnp.where(which == 1, i, j)
                far_y = jnp.where(which == 1, j, i)
                chip = lax.rem(my_x + far_x, side) * side + lax.rem(my_y + far_y, side)
                first = pl.multiple_of((2 * chip + which) * share, share)
                for col in range(width // LANES):
                    out[i, j, col * share : (col + 1) * share, :] = acc[
                        pl.ds(first, share), col * LANES : (col + 1) * LANES
                    ]
                if tail is not None:
                    out[i, j, share * (width // LANES) :, :] = tail


def tail_rows(*sums):
    return jnp.concatenate(
        [each[:, c * LANES : (c + 1) * LANES] for each in sums for c in range(each.shape[1] // LANES)], axis=0
    )


def fold(wide):
    return jnp.sum(wide.reshape(-1, 8, wide.shape[1]), axis=0)


def dot(early, late):
    return lax.dot_general(early, late, CONTRACT, preferred_element_type=F32)


def add_whole(block_ref, first, acc, sums, pair):
    block = block_ref[...]
    acc[...] += dot(block, block)
    if pair is not None:
        pair[0][...] += dot(pair[1][...], block)
    total = fold(block.astype(F32))
    sums[0:8, :] += total
    sums[8:16, :] += total * jnp.where(first >= LAG, 1.0, 0.0)


def add_block(block_ref, first, count, acc, sums, pair):
    full = first + BLK <= count

    @pl.when(full)
    def _():
        add_whole(block_ref, first, acc, sums, pair)

    @pl.when(jnp.logical_and(jnp.logical_not(full), first < count + LAG))
    def _():
        block = block_ref[...]
        wide = block.astype(F32)
        held = jnp.where(rows_below(count - first, wide.shape), wide, 0.0)
        acc[...] += dot(held.astype(block.dtype), block)
        if pair is not None:
            pair[0][...] += dot(keep_below(pair[1][...], count - first + LAG), block)
        later = jnp.where(rows_below(count + LAG - first, wide.shape), wide, 0.0)
        sums[0:8, :] += fold(held)
        sums[8:16, :] += fold(later) * jnp.where(first >= LAG, 1.0, 0.0)


def edges_kernel(place, x_hbm, far_ref, near_ref, sems):
    rows, height = x_hbm.shape[0], far_ref.shape[0]
    parts = sems.shape[0] // 2
    step = height // parts
    copies = []
    for which, out in ((1, far_ref), (0, near_ref)):
        start = jnp.where(place[0] == which, rows - height, 0)
        for k in range(parts):
            source = x_hbm.at[pl.ds(pl.multiple_of(start + k * step, step), step)]
            sem = sems.at[which * parts + k]
            copies.append(pltpu.make_async_copy(source, out.at[pl.ds(k * step, step)], sem))
    for copy in copies:
        copy.start()
    for copy in copies:
        copy.wait()


def moments_kernel(
    place, x_hbm, keep_ref, send_ref, lag, second_ref, late_ref, facts_ref, xs, acc, sums, sems
):
    base, count = place[1], place[2]
    rows = x_hbm.shape[0]
    blocks = rows // BLK
    ahead = LAG // BLK

    def copy(b):
        return pltpu.make_async_copy(x_hbm.at[pl.ds(b * BLK, BLK)], xs.at[b], sems.at[b])

    def again(k, b, out):
        return pltpu.make_async_copy(x_hbm.at[pl.ds(b * BLK, BLK)], out, sems.at[blocks + k])

    kept = [again(0, 1, second_ref), again(1, blocks - ahead, late_ref)]
    for b in range(blocks):
        copy(b).start()
    for each in kept:
        each.start()
    acc[...] = jnp.zeros_like(acc)
    sums[...] = jnp.zeros_like(sums)
    lag[...] = jnp.zeros_like(lag)

    def step(b, with_pair):
        copy(b).wait()
        pair = (lag, xs.at[b - ahead]) if with_pair else None
        add_block(xs.at[b], base + b * BLK, count, acc, sums, pair)

    pl.loop(0, ahead)(lambda b: step(b, False))
    pl.loop(ahead, blocks)(lambda b: step(b, True))
    for each in kept:
        each.wait()
    sum_x = jnp.sum(sums[0:8, :], axis=0, keepdims=True)
    sum_y = jnp.sum(sums[8:16, :], axis=0, keepdims=True)
    write_chunks(place, acc, tail_rows(sum_x, sum_y), keep_ref, send_ref)
    facts_ref[0:8, :] = jnp.full((8, LANES), count, jnp.int32).astype(F32)
    facts_ref[8:16, :] = jnp.full((8, LANES), place[3], jnp.int32).astype(F32)


def border_kernel(far, place, met_ref, second_ref, late_ref, part_ref, *outs):
    core, base, count = place[0], place[1], place[2]
    total = outs[-1]

    def add(first, early_ref, late_ref):
        full = first + BLK <= count

        @pl.when(full)
        def _():
            total[...] = part_ref[...] + dot(early_ref[...], late_ref[...])

        @pl.when(jnp.logical_not(full))
        def _():
            total[...] = part_ref[...] + dot(keep_below(early_ref[...], count - first), late_ref[...])

    @pl.when(core == far)
    def _():
        add(base + place[6] - LAG, late_ref, met_ref)

    @pl.when(core != far)
    def _():
        add(base - BLK, met_ref, second_ref)

    if far:
        write_chunks(place, total, None, outs[0], outs[1])


def pair_kernel(keep_i, met_i, keep_l, met_l, *outs):
    half = keep_i.shape[2]
    for d, out in enumerate(outs):
        out[:, :half, :] = keep_i[d] + met_i[d]
        out[:, half:, :] = keep_l[d] + met_l[d]


def line_kernel(a_ref, b_ref, c_ref, d_ref, *outs):
    for d, out in enumerate(outs):
        out[...] = (a_ref[d] + b_ref[d]) + (c_ref[d] + d_ref[d])


def plane_kernel(facts_ref, a_ref, b_ref, c_ref, d_ref, total_ref):
    height = a_ref.shape[0]
    total_ref[:height, :] = (a_ref[...] + b_ref[...]) + (c_ref[...] + d_ref[...])
    total_ref[height:, :] = facts_ref[0:8, :]


def row_of(rows):
    return jnp.concatenate([rows[c : c + 1, :] for c in range(rows.shape[0])], axis=1)


def centered(total, mean_rows, mean_cols, number, share, out_ref):
    for col in range(out_ref.shape[1] // LANES):
        lanes = slice(col * LANES, (col + 1) * LANES)
        block = total[col * share : (col + 1) * share, :]
        out_ref[:, lanes] = block / number - mean_rows * mean_cols[:, lanes]


def finish(total, facts_ref, inst_ref, lag_ref):
    share, width = inst_ref.shape
    cols = width // LANES
    flat = share * cols
    after = flat + 2 * cols
    number = total[flat + after : flat + after + 1, 0:1]
    mean_x = row_of(total[flat : flat + cols, :]) / number
    mean_y = row_of(total[flat + cols : after, :]) / number
    row = lax.broadcasted_iota(jnp.int32, (share, width), 0)
    col = lax.broadcasted_iota(jnp.int32, (share, width), 1)
    first_row = facts_ref[8:9, 0:1].astype(jnp.int32)
    own = jnp.where(col - row == jnp.broadcast_to(first_row, row.shape), jnp.broadcast_to(mean_x, (share, width)), 0.0)
    mean_rows = jnp.sum(own, axis=1, keepdims=True)
    centered(total[:flat, :], mean_rows, mean_x, number, share, inst_ref)
    centered(total[after : after + flat, :], mean_rows, mean_y, number, share, lag_ref)


def session_kernel(facts_ref, total_ref, inst_ref, lag_ref):
    finish(total_ref[...], facts_ref, inst_ref, lag_ref)


def duo_kernel(a_ref, b_ref, out_ref):
    out_ref[...] = a_ref[...] + b_ref[...]


def pooled_kernel(facts_ref, a_ref, b_ref, inst_ref, lag_ref):
    finish(a_ref[...] + b_ref[...], facts_ref, inst_ref, lag_ref)


def on_device(frames, pair_count):
    local = frames[0]
    rows, width = local.shape
    blocks = rows // BLK
    parts = lax.axis_size("tm")
    sessions = lax.axis_size("group")
    side = math.isqrt(parts // 2)
    share = width // parts
    flat = share * (width // LANES)
    tail = 2 * (width // LANES)
    chunk = 2 * flat + tail
    me = lax.axis_index("tm")
    numbers = [me % 2, me * rows, pair_count[0], me * share, me // (2 * side), (me // 2) % side, rows]
    place = jnp.stack(numbers).astype(jnp.int32)

    smem = pl.BlockSpec(memory_space=pltpu.SMEM)
    vmem = pl.BlockSpec(memory_space=pltpu.VMEM)
    hbm = pl.BlockSpec(memory_space=pl.ANY)
    params = pltpu.CompilerParams(vmem_limit_bytes=VMEM_LIMIT)

    def floats(*shape):
        return jax.ShapeDtypeStruct(shape, F32)

    def call(kernel, name, ins, out_shape, scratch=(), flops=0, moved=0):
        specs = jax.tree.map(lambda _: vmem, out_shape)
        return pl.pallas_call(
            kernel,
            out_shape=out_shape,
            in_specs=[spec for _, spec in ins],
            out_specs=specs,
            scratch_shapes=list(scratch),
            compiler_params=params,
            cost_estimate=pl.CostEstimate(flops=flops, bytes_accessed=moved, transcendentals=0),
            name=name,
        )(*[operand for operand, _ in ins])

    def dma(n):
        return pltpu.SemaphoreType.DMA((n,))

    where, frames_in = (place, smem), (local, hbm)
    edge = jax.ShapeDtypeStruct((BLK, width), local.dtype)
    swap = [(i, i ^ 1) for i in range(parts)]
    cross = [(i, i + 1 if i % 2 else i - 1) for i in range(1, parts - 1)]

    far, near = call(edges_kernel, "edges", [where, frames_in], (edge, edge), [dma(8)], 0, 4 * BLK * width)
    far = lax.ppermute(far, "tm", cross)
    near = lax.ppermute(near, "tm", swap)

    def at(x, y, c):
        return ((x % side) * side + y % side) * 2 + c

    def gather(blocks, stage):
        came = [blocks[0]]
        for d in range(1, side):
            route = []
            for x in range(side):
                for y in range(side):
                    for c in range(2):
                        on_x = c != stage
                        route.append((at(x, y, c), at(x + d * on_x, y + d * (not on_x), c)))
            came.append(lax.ppermute(blocks[d], "tm", route))
        return came

    square = pltpu.VMEM((width, width), F32)
    held = pltpu.VMEM((blocks, BLK, width), local.dtype)
    work = 2 * rows * width * width
    keep_i, send_i, partial, second, late, facts = call(
        moments_kernel,
        "moments",
        [where, frames_in],
        (*[floats(side, side, flat + tail, LANES)] * 2, floats(width, width), edge, edge, floats(16, LANES)),
        [held, square, pltpu.VMEM((16, width), F32), dma(blocks + 2)],
        work * 7 // 4,
        rows * width * 2,
    )
    partial = call(
        functools.partial(border_kernel, 0),
        "border_near",
        [where, *[(v, vmem) for v in (near, second, late, partial)]],
        floats(width, width),
        (),
        work // 8,
        rows * width,
    )
    keep_l, send_l = call(
        functools.partial(border_kernel, 1),
        "border_far",
        [where, *[(v, vmem) for v in (far, second, late, partial)]],
        [floats(side, side, flat, LANES)] * 2,
        [square],
        work // 8,
        rows * width,
    )
    met_i = lax.ppermute(send_i, "tm", swap)
    met_l = lax.ppermute(send_l, "tm", swap)

    def all_vmem(values):
        return [(v, vmem) for v in values]

    both = floats(side, chunk, LANES)
    lines = call(pair_kernel, "pair", all_vmem((keep_i, met_i, keep_l, met_l)), [both] * side)
    cells = call(line_kernel, "line", all_vmem(gather(lines, 0)), [floats(chunk, LANES)] * side)
    whole = floats(chunk + 8, LANES)
    total = call(plane_kernel, "plane", all_vmem((facts, *gather(cells, 1))), whole)
    out = floats(share, width)
    group_instant, group_lagged = call(session_kernel, "session", all_vmem((facts, total)), (out, out))
    for route in (lambda i: i ^ 1, lambda i: i ^ 2, lambda i: (sessions - 2 - (i & -2)) | (i & 1)):
        other = lax.ppermute(total, "group", [(i, route(i)) for i in range(sessions)])
        last = (total, other)
        total = call(duo_kernel, "duo", all_vmem(last), whole)
    pooled_instant, pooled_lagged = call(
        pooled_kernel, "pooled", all_vmem((facts, *last)), (out, out)
    )
    return (group_instant[None], group_lagged[None], pooled_instant, pooled_lagged)


def solution(mesh):
    in_specs = (P("group", "tm", None), P("group"))
    out_specs = (P("group", "tm", None), P("group", "tm", None), P("tm", None), P("tm", None))
    return jax.shard_map(
        on_device, mesh=mesh, in_specs=in_specs, out_specs=out_specs, check_vma=False
    )
```
